32 devices in a mesh: kv: 4 (over y, x), tok: 8 (over z, core).
Axes of the slice: x: 2, y: 2, z: 4, core: 2. Of those that a mesh axis runs over, the one named last changes fastest.
Arguments:
- dec_tokens: bfloat16 [128, 5120], P('tok', 'kv'), may hold values from -60 to 60
- pre_tokens: bfloat16 [2048, 5120], P('tok', 'kv'), may hold values from -60 to 60
- w_query: bfloat16 [5120, 2560], P(None, 'kv'), may hold values from -0.078125 to 0.078125
- w_keyval: bfloat16 [5120, 2, 512], P(None, None, 'kv'), may hold values from -0.078125 to 0.078125
- b_query: float32 [2560], P('kv'), may hold values from -3 to 3
- b_keyval: float32 [2, 512], P(None, 'kv'), may hold values from -3 to 3
- dec_pool: bfloat16 [2, 98304, 512], P(None, 'tok', 'kv'), may hold values from -72 to 72
- owner_slots: int32 [128], P('tok'), may hold values from 0 to 127, each once
- dec_lengths: int32 [128], P('tok'), may hold values from 1 to 4096, as said below
- pre_cache: bfloat16 [2, 8192, 512], P(None, 'tok', 'kv'), may hold values from -72 to 72
- pre_offsets: int32 [4], replicated, may hold values from 1536 to 2048
Outputs:
- dec_attn: bfloat16 [128, 2560], P('tok', 'kv')
- pre_attn: bfloat16 [2048, 2560], P('tok', 'kv')
- new_pool: bfloat16 [2, 98304, 512], P(None, 'tok', 'kv')
- pre_keyval: bfloat16 [2, 2048, 512], P(None, 'tok', 'kv')
The draws below stay inside these ranges and needn't reach their ends.
Inputs may be any that keep to these rules, and one draw needn't show every extreme that they name: `dec_lengths`: in the 16 slots of each owner, one length is 512 or more and the others are below 512, so an owner's lengths plus one each sum to at most 12288.
All inputs are finite; a program needn't handle non-finite values.
Results may differ from the reference program's by a relative error of at most 0.0065.
The reference program's roundings to bfloat16 on the way count: a program that leaves them out, or rounds other values in their place, can miss the bound.
Values may be sent and summed in bfloat16 or wider, within the bound.
A program may use at most 128 MiB of HBM per device.

```python
import jax
import jax.numpy as jnp
from jax import lax

D = 5120
HD = 128
QH = 20
KVH = 4
BLOCK = 512
PSH = 1024
LMAX = 4096
SHORT = 512
DEC_DEV = 16
DEC = 128
PRE = 4
DPOOL = 12288
N_TOK = 8


def token_rows(key, amount):
    first_key = jax.random.fold_in(key, 0)
    values = jax.random.truncated_normal(first_key, -6.0, 6.0, (amount, D), jnp.float32)
    return values.astype(jnp.bfloat16)


def cache_rows(key, length):
    first_key = jax.random.fold_in(key, 0)
    values = jax.random.truncated_normal(first_key, -6.0, 6.0, (2, length, KVH * HD), jnp.float32)
    return values.astype(jnp.bfloat16)


def draw_dec_tokens(key, part):
    return token_rows(key, DEC)


def draw_pre_tokens(key, part):
    return token_rows(key, PRE * BLOCK)


def draw_dec_pool(key, part):
    return cache_rows(key, DEC // DEC_DEV * DPOOL)


def draw_pre_cache(key, part):
    return cache_rows(key, PRE * 2 * PSH)


def draw_dec_lengths(key, part):
    keys_list = jax.random.split(key, 5)
    owner_count = DEC // DEC_DEV
    ceilings = jax.random.randint(keys_list[0], (owner_count, DEC_DEV), 2, SHORT + 1)
    short_len = jax.random.randint(keys_list[1], (owner_count, DEC_DEV), 1, ceilings)
    long_len = jax.random.randint(keys_list[2], (owner_count, 1), SHORT, LMAX + 1)
    picked = jax.random.randint(keys_list[3], (), 0, owner_count)
    long_len = jnp.where(jnp.arange(owner_count)[:, None] == picked, LMAX, long_len)
    long_slot = jax.random.randint(keys_list[4], (owner_count, 1), 0, DEC_DEV)
    lengths = jnp.where(jnp.arange(DEC_DEV)[None, :] == long_slot, long_len, short_len)
    return lengths.reshape(DEC).astype(jnp.int32)


def draw_pre_offsets(key, part):
    first_key, second_key = jax.random.split(key)
    offsets = jax.random.randint(first_key, (PRE,), PSH + PSH // 2, 2 * PSH + 1)
    picked = jax.random.randint(second_key, (), 0, PRE)
    return jnp.where(jnp.arange(PRE) == picked, 2 * PSH, offsets).astype(jnp.int32)


def level_of(own_key, extent, cuts, smallest, top_value):
    factor_of = 1.0
    for dim, blocks in cuts:
        heights = jax.random.uniform(jax.random.fold_in(jax.random.fold_in(own_key, 6), dim), (blocks,), jnp.float32, smallest / len(cuts), top_value / len(cuts))
        factor_of = factor_of * jnp.repeat(jnp.exp(heights), extent[dim] // blocks).reshape((-1,) + (1,) * (len(extent) - 1 - dim))
    return factor_of


def noise(key, extent, scale, limit, cuts=(), held_as=jnp.bfloat16):
    drawn = scale * jax.random.normal(key, extent, jnp.float32)
    if cuts:
        drawn = drawn * level_of(key, extent, cuts, -0.22, 0.18)
    return jnp.clip(drawn, -limit, limit).astype(held_as)


def setup_inputs(seed: int = 0) -> dict:
    key_of = jax.random.split(jax.random.key(seed), 12)
    return {
        "dec_tokens": draw_dec_tokens(jax.random.fold_in(key_of[11], 71), 0),
        "pre_tokens": draw_pre_tokens(jax.random.fold_in(key_of[11], 71), 0),
        "w_query": noise(key_of[2], (D, QH * HD), D ** -0.5, 0.078125, ((1, 4),)),
        "w_keyval": noise(key_of[3], (D, 2, KVH * HD), D ** -0.5, 0.078125, ((2, 4),)),
        "b_query": noise(key_of[4], (QH * HD,), 0.5, 3.0, ((0, 4),), jnp.float32),
        "b_keyval": noise(key_of[5], (2, KVH * HD), 0.5, 3.0, ((1, 4),), jnp.float32),
        "dec_pool": draw_dec_pool(jax.random.fold_in(key_of[11], 71), 0),
        "owner_slots": jax.random.permutation(key_of[7], DEC).astype(jnp.int32),
        "dec_lengths": draw_dec_lengths(jax.random.fold_in(key_of[11], 71), 0),
        "pre_cache": draw_pre_cache(jax.random.fold_in(key_of[11], 71), 0),
        "pre_offsets": draw_pre_offsets(jax.random.fold_in(key_of[11], 71), 0),
    }


THETA = 1000000.0


def rotate(values, positions):
    halfway = values.shape[-1] // 2
    spread = jnp.arange(halfway, dtype=jnp.float32) * (2.0 / values.shape[-1])
    rates = jnp.power(jnp.float32(THETA), -spread)
    angles = positions.astype(jnp.float32)[:, None] * rates[None, :]
    cosine = jnp.cos(angles)[:, None, :]
    sine = jnp.sin(angles)[:, None, :]
    former = values[..., :halfway]
    latter = values[..., halfway:]
    return jnp.concatenate([former * cosine - latter * sine, latter * cosine + former * sine], axis=-1)


def head_scores(queries, key_rows, allowed):
    amount = queries.shape[0]
    q_heads = queries.shape[1] // HD
    kv_heads = key_rows.shape[1] // HD
    per_group = q_heads // kv_heads
    shaped = queries.reshape(amount, q_heads, HD).astype(jnp.float32)
    pieces = []
    for kv_head in range(kv_heads):
        product = jnp.einsum("ngd,md->ngm", shaped[:, kv_head * per_group:(kv_head + 1) * per_group],
                             key_rows[:, kv_head * HD:(kv_head + 1) * HD].astype(jnp.float32))
        pieces.append(product)
    scores = jnp.concatenate(pieces, axis=1) * (HD ** -0.5)
    return jnp.where(allowed[:, None, :], scores, -jnp.inf)


def head_mix(scores, peaks, value_rows):
    powers = jnp.exp(scores - peaks[..., None])
    totals = jnp.sum(powers, axis=-1)
    weights = powers.astype(jnp.bfloat16)
    kv_heads = value_rows.shape[1] // HD
    per_group = scores.shape[1] // kv_heads
    pieces = []
    for kv_head in range(kv_heads):
        product = jnp.einsum("ngm,md->ngd", weights[:, kv_head * per_group:(kv_head + 1) * per_group].astype(jnp.float32),
                             value_rows[:, kv_head * HD:(kv_head + 1) * HD].astype(jnp.float32))
        pieces.append(product)
    return totals, jnp.concatenate(pieces, axis=1)


def serve_owner(queries, keyval, lengths, cache_pool):
    amount = queries.shape[0]
    q_heads = queries.shape[1] // HD
    kv_heads = cache_pool.shape[2] // HD
    finish = jnp.cumsum(lengths + 1).astype(jnp.int32)
    starts = (finish - lengths - 1).astype(jnp.int32)
    turned = rotate(queries.astype(jnp.float32).reshape(amount, q_heads, HD), lengths)
    turned = turned.astype(jnp.bfloat16).reshape(amount, q_heads * HD)
    new_keys = rotate(keyval[:, 0].astype(jnp.float32).reshape(amount, kv_heads, HD), lengths)
    new_keys = new_keys.astype(jnp.bfloat16).reshape(amount, kv_heads * HD)
    appended = jnp.stack([new_keys, keyval[:, 1]], axis=0)
    cache_pool = cache_pool.at[:, starts + lengths].set(appended)
    spots = jnp.arange(cache_pool.shape[1], dtype=jnp.int32)
    allowed = (spots[None, :] >= starts[:, None]) & (spots[None, :] <= (starts + lengths)[:, None])
    scores = head_scores(turned, cache_pool[0], allowed)
    totals, mixed = head_mix(scores, jnp.max(scores, axis=-1), cache_pool[1])
    result = (mixed / totals[..., None]).astype(jnp.bfloat16).reshape(amount, q_heads * HD)
    return result, cache_pool


def reference(dec_tokens, pre_tokens, w_query, w_keyval, b_query, b_keyval, dec_pool, owner_slots, dec_lengths, pre_cache, pre_offsets):
    width = w_keyval.shape[2]
    kv_weight = w_keyval.reshape(w_keyval.shape[0], 2 * width)
    kv_bias = b_keyval.reshape(2 * width)
    dec_query = (jnp.dot(dec_tokens, w_query, preferred_element_type=jnp.float32) + b_query).astype(jnp.bfloat16)
    dec_keyval = (jnp.dot(dec_tokens, kv_weight, preferred_element_type=jnp.float32) + kv_bias).astype(jnp.bfloat16)
    dec_query = lax.optimization_barrier(dec_query)
    dec_keyval = lax.optimization_barrier(dec_keyval).reshape(DEC, 2, width)

    def serve(owner_id):
        chosen = lax.dynamic_slice_in_dim(owner_slots, owner_id * DEC_DEV, DEC_DEV)
        lengths = lax.dynamic_slice_in_dim(dec_lengths, owner_id * DEC_DEV, DEC_DEV)
        cache_pool = lax.dynamic_slice_in_dim(dec_pool, owner_id * DPOOL, DPOOL, axis=1)
        return serve_owner(jnp.take(dec_query, chosen, axis=0), jnp.take(dec_keyval, chosen, axis=0), lengths, cache_pool)

    results, new_pools = lax.map(serve, jnp.arange(N_TOK, dtype=jnp.int32))
    dec_attn = jnp.zeros((DEC, QH * HD), jnp.bfloat16).at[owner_slots].set(results.reshape(DEC, QH * HD))
    new_pool = jnp.transpose(new_pools, (1, 0, 2, 3)).reshape(2, N_TOK * DPOOL, width)

    pre_query = jnp.dot(pre_tokens, w_query, preferred_element_type=jnp.float32) + b_query
    pre_kv = (jnp.dot(pre_tokens, kv_weight, preferred_element_type=jnp.float32) + kv_bias).reshape(PRE * BLOCK, 2, width)

    def prefill(prefill_id):
        offset = pre_offsets[prefill_id]
        positions = offset + jnp.arange(BLOCK, dtype=jnp.int32)
        queries = lax.dynamic_slice_in_dim(pre_query, prefill_id * BLOCK, BLOCK)
        keyval = lax.dynamic_slice_in_dim(pre_kv, prefill_id * BLOCK, BLOCK)
        turned = rotate(queries.reshape(BLOCK, QH, HD), positions).astype(jnp.bfloat16).reshape(BLOCK, QH * HD)
        new_keys = rotate(keyval[:, 0].reshape(BLOCK, KVH, HD), positions).astype(jnp.bfloat16).reshape(BLOCK, width)
        appended = jnp.stack([new_keys, keyval[:, 1].astype(jnp.bfloat16)], axis=0)
        history = lax.dynamic_slice_in_dim(pre_cache, prefill_id * 2 * PSH, 2 * PSH, axis=1)
        key_rows = jnp.concatenate([history, appended], axis=1)
        key_slots = jnp.arange(2 * PSH + BLOCK, dtype=jnp.int32)
        key_pos = jnp.where(key_slots < 2 * PSH, key_slots, offset + key_slots - 2 * PSH)
        usable = (key_slots < offset) | (key_slots >= 2 * PSH)
        allowed = usable[None, :] & (key_pos[None, :] <= positions[:, None])
        scores = head_scores(turned, key_rows[0], allowed)
        totals, mixed = head_mix(scores, jnp.max(scores, axis=-1), key_rows[1])
        return (mixed / totals[..., None]).astype(jnp.bfloat16).reshape(BLOCK, QH * HD), appended

    pre_results, pre_new = lax.map(prefill, jnp.arange(PRE, dtype=jnp.int32))
    pre_attn = pre_results.reshape(PRE * BLOCK, QH * HD)
    pre_keyval = jnp.transpose(pre_new, (1, 0, 2, 3)).reshape(2, PRE * BLOCK, width)
    return dec_attn, pre_attn, new_pool, pre_keyval
```

```python
import functools

import jax
import jax.numpy as jnp
import numpy as np
from jax import lax
from jax.experimental import pallas as pl
from jax.experimental.pallas import tpu as pltpu
from jax.sharding import PartitionSpec as P

HD = 128
THETA = 1000000.0
MESH = pl.DeviceIdType.MESH
CHUNKS = 4
F32 = jnp.float32
BF16 = jnp.bfloat16


def rotated(value, cosine, sine):
    return value * cosine + pltpu.roll(value, HD // 2, 1) * sine


def dot_nt(a, b):
    return lax.dot_general(a, b, (((1,), (1,)), ((), ())), preferred_element_type=F32)


def step_kernel(
    n_tok,
    dec_x, pre_x, w_q, w_kv, b_q, b_kv, pool, slots, lengths, cache, offsets, rates,
    o_dec, o_pre, o_kv, o_new,
    xd, xp, w, raw, kvpool, hist, nk, qs, ms, ls, acc, dq_own, dq_all, dr_send, dr_recv,
    l_sem, ds_sem, dr_sem, ps_sem, pr_sem, qs_sem, qr_sem, rs_sem, rr_sem,
    cs_sem, cr_sem, ks_sem, kr_sem,
):
    kv = lax.axis_index("kv")
    tok = lax.axis_index("tok")
    mate = tok + 1 - 2 * lax.rem(tok, 2)
    half = lax.rem(tok, 2)
    px = kv + 1 - 2 * lax.rem(kv, 2)
    py = lax.rem(kv + 2, 4)
    pd = lax.rem(px + 2, 4)
    dec_rows, width = dec_x.shape
    pre_rows = pre_x.shape[0]
    q_width = w_q.shape[1]
    heads = q_width // HD
    rows = pre_rows // CHUNKS
    mid = rows // 2
    shard = cache.shape[1]
    scale = HD ** -0.5

    loads = [
        pltpu.make_async_copy(w_kv, raw, l_sem.at[0]),
        pltpu.make_async_copy(w_q, w.at[:, pl.ds(0, q_width)], l_sem.at[1]),
        pltpu.make_async_copy(dec_x, xd.at[kv], l_sem.at[2]),
        pltpu.make_async_copy(pre_x, xp.at[kv], l_sem.at[3]),
        pltpu.make_async_copy(
            cache, hist.at[:, pl.ds(pl.multiple_of(half * shard, shard), shard)], l_sem.at[4]
        ),
        pltpu.make_async_copy(pool, kvpool, l_sem.at[5]),
    ]
    for load in loads:
        load.start()

    barrier = pltpu.get_barrier_semaphore()
    for peer in (px, py, pd):
        pl.semaphore_signal(barrier, inc=1, device_id=(peer, tok), device_id_type=MESH)
    for d in range(1, n_tok):
        pl.semaphore_signal(
            barrier, inc=1, device_id=(kv, lax.rem(tok + d, n_tok)), device_id_type=MESH
        )
    pl.semaphore_wait(barrier, n_tok + 2)

    def remote(src, dst, send, recv, where):
        return pltpu.make_async_remote_copy(
            src_ref=src, dst_ref=dst, send_sem=send, recv_sem=recv,
            device_id=where, device_id_type=MESH,
        )

    dec_sends = [
        remote(dec_x, xd.at[kv], ds_sem.at[i], dr_sem.at[i], (peer, tok))
        for i, peer in enumerate((px, py, pd))
    ]
    for send in dec_sends:
        send.start()

    def own_sends(r):
        part = pl.ds(r * rows, rows)
        return [
            remote(pre_x.at[part], xp.at[kv, part], ps_sem.at[r, i], pr_sem.at[r, i], (peer, tok))
            for i, peer in enumerate((px, py))
        ]

    def forwards(r):
        first, second = pl.ds(r * rows, mid), pl.ds(r * rows + mid, mid)
        return [
            remote(xp.at[py, first], xp.at[py, first], ps_sem.at[r, 2], pr_sem.at[r, 2], (px, tok)),
            remote(xp.at[px, second], xp.at[px, second], ps_sem.at[r, 3], pr_sem.at[r, 3], (py, tok)),
        ]

    own = [own_sends(r) for r in range(CHUNKS)]
    onward = [forwards(r) for r in range(CHUNKS)]
    for r in range(2):
        for send in own[r]:
            send.start()
    hist_part = hist.at[:, pl.ds(pl.multiple_of(half * shard, shard), shard)]
    cache_send = remote(cache, hist_part, cs_sem, cr_sem, (kv, mate))
    cache_send.start()

    def pump(r):
        for send in own[r]:
            send.wait_recv()
        for send in onward[r]:
            send.start()
        if r + 2 < CHUNKS:
            for send in own[r + 2]:
                send.start()

    loads[0].wait()
    block = 512
    row = lax.broadcasted_iota(jnp.int32, (block, block), 0)
    col = lax.broadcasted_iota(jnp.int32, (block, block), 1)
    wanted = jnp.where(row < block // 2, 2 * row, 2 * row - block + 1)
    permute = jnp.where(col == wanted, 1.0, 0.0).astype(BF16)

    def part_weights(i, carry):
        tile = raw[pl.ds(pl.multiple_of(i * block, block), block), :]
        parted = jnp.dot(permute, tile, preferred_element_type=F32).astype(BF16)
        where = pl.ds(pl.multiple_of(i * (block // 2), block // 2), block // 2)
        w[where, pl.ds(q_width, HD)] = parted[: block // 2]
        w[where, pl.ds(q_width + HD, HD)] = parted[block // 2:]
        return carry

    lax.fori_loop(0, raw.shape[0] // block, part_weights, 0)

    def project(x_ref, start, amount):
        def add(s, total):
            return total + jnp.dot(
                x_ref[s, pl.ds(start, amount), :],
                w[pl.ds(pl.multiple_of(s * width, width), width), :],
                preferred_element_type=F32,
            )

        total = lax.fori_loop(0, 4, add, jnp.zeros((amount, q_width + 2 * HD), F32))
        bias = jnp.concatenate([b_q[...], b_kv[0:1, :], b_kv[1:2, :]], axis=1)
        return total + bias

    loads[1].wait()
    loads[2].wait()
    for send in dec_sends:
        send.wait_recv()
    dq_own[...] = project(xd, 0, dec_rows).astype(BF16)
    q_sends = [
        remote(dq_own, dq_all.at[tok], qs_sem.at[d - 1], qr_sem.at[d - 1],
               (kv, lax.rem(tok + d, n_tok)))
        for d in range(1, n_tok)
    ]
    for send in q_sends:
        send.start()
    dq_all[tok] = dq_own[...]

    pump(0)
    pump(1)

    for send in q_sends:
        send.wait_recv()
    requests = n_tok * dec_rows
    row = lax.broadcasted_iota(jnp.int32, (dec_rows, requests), 0)
    col = lax.broadcasted_iota(jnp.int32, (dec_rows, requests), 1)
    row_t = lax.broadcasted_iota(jnp.int32, (requests, dec_rows), 0)
    col_t = lax.broadcasted_iota(jnp.int32, (requests, dec_rows), 1)
    stacked = heads * dec_rows
    slot_of = lax.rem(lax.broadcasted_iota(jnp.int32, (stacked, 1), 0), dec_rows)
    line = lax.broadcasted_iota(jnp.int32, (dec_rows, HD), 0)
    chosen = jnp.zeros((dec_rows, requests), F32)
    chosen_t = jnp.zeros((requests, dec_rows), F32)
    first = jnp.zeros((stacked, 1), jnp.int32)
    last = jnp.zeros((stacked, 1), jnp.int32)
    places = jnp.zeros((dec_rows, HD), jnp.int32)
    begin = jnp.int32(0)
    for s in range(dec_rows):
        request = slots[s]
        length = lengths[s]
        chosen = jnp.where((row == s) & (col == request), 1.0, chosen)
        chosen_t = jnp.where((col_t == s) & (row_t == request), 1.0, chosen_t)
        first = jnp.where(slot_of == s, begin, first)
        last = jnp.where(slot_of == s, begin + length, last)
        places = jnp.where(line == s, length, places)
        begin = begin + length + 1
    chosen = chosen.astype(BF16)
    chosen_t = chosen_t.astype(BF16)
    every = dq_all[...].reshape(requests, q_width + 2 * HD)
    mine = jnp.dot(chosen, every, preferred_element_type=F32)
    lane = lax.broadcasted_iota(jnp.int32, (1, HD), 1)
    sign = jnp.where(lane < HD // 2, -1.0, 1.0)
    angles = places.astype(F32) * rates[...]
    cosine = jnp.cos(angles)
    sine = jnp.sin(angles) * sign
    turned = jnp.concatenate(
        [rotated(mine[:, h * HD:(h + 1) * HD], cosine, sine) for h in range(heads)], axis=0
    ).astype(BF16)
    fresh_k = rotated(mine[:, q_width:q_width + HD], cosine, sine).astype(BF16)
    fresh_v = mine[:, q_width + HD:].astype(BF16)
    o_new[0] = fresh_k
    o_new[1] = fresh_v
    same = slot_of == lax.broadcasted_iota(jnp.int32, (stacked, dec_rows), 1)
    scores = jnp.where(same, dot_nt(turned, fresh_k) * scale, -jnp.inf)
    peak = jnp.max(scores, axis=1, keepdims=True)
    powers = jnp.exp(scores - peak)
    total = jnp.sum(powers, axis=1, keepdims=True)
    mixed = jnp.dot(powers.astype(BF16), fresh_v, preferred_element_type=F32)
    loads[5].wait()
    tile = 2048

    def visit(t, carry):
        peak, total, mixed = carry
        where = pl.ds(pl.multiple_of(t * tile, tile), tile)
        spots = t * tile + lax.broadcasted_iota(jnp.int32, (stacked, tile), 1)
        scores = dot_nt(turned, kvpool[0, where, :]) * scale
        scores = jnp.where((spots >= first) & (spots < last), scores, -jnp.inf)
        top = jnp.maximum(peak, jnp.max(scores, axis=1, keepdims=True))
        powers = jnp.exp(scores - top)
        fade = jnp.exp(peak - top)
        total = total * fade + jnp.sum(powers, axis=1, keepdims=True)
        mixed = mixed * fade + jnp.dot(
            powers.astype(BF16), kvpool[1, where, :], preferred_element_type=F32
        )
        return top, total, mixed

    peak, total, mixed = lax.fori_loop(0, pool.shape[1] // tile, visit, (peak, total, mixed))
    result = (mixed / total).astype(BF16)
    result = jnp.concatenate(
        [result[h * dec_rows:(h + 1) * dec_rows] for h in range(heads)], axis=1
    )
    spread = jnp.dot(chosen_t, result, preferred_element_type=F32).astype(BF16)
    dr_send[...] = spread.reshape(n_tok, dec_rows, q_width)
    r_sends = []
    for d in range(1, n_tok):
        peer = lax.rem(tok + d, n_tok)
        r_sends.append(
            remote(dr_send.at[peer], dr_recv.at[tok], rs_sem.at[d - 1], rr_sem.at[d - 1],
                   (kv, peer))
        )
    for send in r_sends:
        send.start()
    dr_recv[tok] = dr_send[tok]
    pump(2)

    offset = offsets[lax.div(tok, 2)]
    loads[3].wait()
    loads[4].wait()
    cache_send.wait_recv()
    key_sends = []
    for r in range(CHUNKS):
        for send in onward[r]:
            send.wait_recv()
        value = project(xp, r * rows, rows)
        place = pl.multiple_of(half * pre_rows + r * rows, rows)
        positions = offset + place + lax.broadcasted_iota(jnp.int32, (rows, HD), 0)
        angles = positions.astype(F32) * rates[...]
        cosine = jnp.cos(angles)
        sine = jnp.sin(angles) * sign
        queries = jnp.concatenate(
            [rotated(value[:, h * HD:(h + 1) * HD], cosine, sine) for h in range(heads)], axis=0
        ).astype(BF16)
        qs[r] = queries
        new_k = rotated(value[:, q_width:q_width + HD], cosine, sine).astype(BF16)
        new_v = value[:, q_width + HD:].astype(BF16)
        o_kv[0, pl.ds(r * rows, rows), :] = new_k
        o_kv[1, pl.ds(r * rows, rows), :] = new_v
        nk[0, pl.ds(place, rows), :] = new_k
        nk[1, pl.ds(place, rows), :] = new_v
        part = nk.at[:, pl.ds(place, rows)]
        send = remote(part, part, ks_sem.at[r], kr_sem.at[r], (kv, mate))
        send.start()
        key_sends.append(send)
        if r == 0:
            pump(3)
        scores = dot_nt(queries, hist[0]) * scale
        cached = lax.broadcasted_iota(jnp.int32, (1, 2 * shard), 1) < offset
        scores = jnp.where(cached, scores, -jnp.inf)
        peak = jnp.max(scores, axis=1, keepdims=True)
        powers = jnp.exp(scores - peak)
        total = jnp.sum(powers, axis=1, keepdims=True)
        acc[r] = jnp.dot(powers.astype(BF16), hist[1], preferred_element_type=F32)
        ms[r] = jnp.broadcast_to(peak, (heads * rows, HD))
        ls[r] = jnp.broadcast_to(total, (heads * rows, HD))

    for send in r_sends:
        send.wait_recv()
    gathered = dr_recv[0].astype(F32)
    for o in range(1, n_tok):
        gathered = gathered + dr_recv[o].astype(F32)
    o_dec[...] = gathered.astype(BF16)

    for send in key_sends:
        send.wait_recv()
    inner = lax.rem(lax.broadcasted_iota(jnp.int32, (heads * rows, 1), 0), rows)
    later = lax.broadcasted_iota(jnp.int32, (heads * rows, 2 * pre_rows), 1)

    def finish(r, carry):
        scores = dot_nt(qs[r], nk[0]) * scale
        scores = jnp.where(later <= inner + (half * pre_rows + r * rows), scores, -jnp.inf)
        peak = ms[r][:, :1]
        top = jnp.maximum(peak, jnp.max(scores, axis=1, keepdims=True))
        powers = jnp.exp(scores - top)
        fade = jnp.exp(peak - top)
        total = ls[r][:, :1] * fade + jnp.sum(powers, axis=1, keepdims=True)
        mixed = acc[r] * fade + jnp.dot(powers.astype(BF16), nk[1], preferred_element_type=F32)
        result = (mixed / total).astype(BF16)
        for h in range(heads):
            o_pre[pl.ds(pl.multiple_of(r * rows, rows), rows), h * HD:(h + 1) * HD] = (
                result[h * rows:(h + 1) * rows]
            )
        return carry

    lax.fori_loop(0, CHUNKS, finish, 0)

    for send in dec_sends + q_sends + r_sends + key_sends + [cache_send]:
        send.wait_send()
    for r in range(CHUNKS):
        for send in own[r] + onward[r]:
            send.wait_send()


def pool_kernel(pool, fresh, lengths, out, buffer, in_sem, out_sem):
    parts = 4
    size = pool.shape[1] // parts
    pieces = [(c, pl.ds(i * size, size)) for c in range(2) for i in range(parts)]
    reads = [
        pltpu.make_async_copy(pool.at[c, p], buffer.at[c, p], in_sem.at[i])
        for i, (c, p) in enumerate(pieces)
    ]
    writes = [
        pltpu.make_async_copy(buffer.at[c, p], out.at[c, p], out_sem.at[i])
        for i, (c, p) in enumerate(pieces)
    ]
    for copy in reads:
        copy.start()
    for copy in reads:
        copy.wait()
    line = lax.broadcasted_iota(jnp.int32, (16, HD), 0)
    end = jnp.int32(0)
    for s in range(fresh.shape[1]):
        end = end + lengths[s]
        base = pl.multiple_of(lax.div(end, 16) * 16, 16)
        for c in range(2):
            new_row = fresh[c, s:s + 1, :].astype(F32)
            held = buffer[c, pl.ds(base, 16), :].astype(F32)
            buffer[c, pl.ds(base, 16), :] = jnp.where(
                line == end - base, new_row, held
            ).astype(BF16)
        end = end + 1
    for copy in writes:
        copy.start()
    for copy in writes:
        copy.wait()


def body(
    n_tok, dec_tokens, pre_tokens, w_query, w_keyval, b_query, b_keyval,
    dec_pool, owner_slots, dec_lengths, pre_cache, pre_offsets,
):
    dec_rows, width = dec_tokens.shape
    pre_rows = pre_tokens.shape[0]
    q_width = w_query.shape[1]
    heads = q_width // HD
    depth = w_query.shape[0]
    out_width = q_width + 2 * HD
    rows = pre_rows // CHUNKS
    shard = pre_cache.shape[1]
    spread = np.arange(HD // 2, dtype=np.float32) * np.float32(2.0 / HD)
    rates = np.power(np.float32(THETA), -spread).astype(np.float32)
    rates = jnp.asarray(np.concatenate([rates, rates])[None, :])
    hbm = pl.BlockSpec(memory_space=pl.ANY)
    vmem = pl.BlockSpec(memory_space=pltpu.VMEM)
    smem = pl.BlockSpec(memory_space=pltpu.SMEM)
    dma = pltpu.SemaphoreType.DMA
    dec_attn, pre_attn, appended, fresh = pl.pallas_call(
        functools.partial(step_kernel, n_tok),
        name="attention_step",
        out_shape=(
            jax.ShapeDtypeStruct((dec_rows, q_width), BF16),
            jax.ShapeDtypeStruct((pre_rows, q_width), BF16),
            jax.ShapeDtypeStruct((2, pre_rows, HD), BF16),
            jax.ShapeDtypeStruct((2, dec_rows, HD), BF16),
        ),
        in_specs=[hbm, hbm, hbm, hbm, vmem, vmem, hbm, smem, smem, hbm, smem, vmem],
        out_specs=(vmem, vmem, vmem, vmem),
        scratch_shapes=[
            pltpu.VMEM((4, dec_rows, width), BF16),
            pltpu.VMEM((4, pre_rows, width), BF16),
            pltpu.VMEM((depth, out_width), BF16),
            pltpu.VMEM((2 * depth, HD), BF16),
            pltpu.VMEM(dec_pool.shape, BF16),
            pltpu.VMEM((2, 2 * shard, HD), BF16),
            pltpu.VMEM((2, 2 * pre_rows, HD), BF16),
            pltpu.VMEM((CHUNKS, heads * rows, HD), BF16),
            pltpu.VMEM((CHUNKS, heads * rows, HD), F32),
            pltpu.VMEM((CHUNKS, heads * rows, HD), F32),
            pltpu.VMEM((CHUNKS, heads * rows, HD), F32),
            pltpu.VMEM((dec_rows, out_width), BF16),
            pltpu.VMEM((n_tok, dec_rows, out_width), BF16),
            pltpu.VMEM((n_tok, dec_rows, q_width), BF16),
            pltpu.VMEM((n_tok, dec_rows, q_width), BF16),
            dma((6,)),
            dma((3,)), dma((3,)),
            dma((CHUNKS, 4)), dma((CHUNKS, 4)),
            dma((n_tok - 1,)), dma((n_tok - 1,)),
            dma((n_tok - 1,)), dma((n_tok - 1,)),
            dma, dma,
            dma((CHUNKS,)), dma((CHUNKS,)),
        ],
        compiler_params=pltpu.CompilerParams(
            collective_id=0, has_side_effects=True, vmem_limit_bytes=52 * 1024 * 1024
        ),
    )(
        dec_tokens, pre_tokens, w_query, w_keyval.reshape(2 * depth, HD),
        b_query.reshape(1, q_width), b_keyval, dec_pool, owner_slots, dec_lengths,
        pre_cache, pre_offsets, rates,
    )
    new_pool = pl.pallas_call(
        pool_kernel,
        name="append_rows",
        out_shape=jax.ShapeDtypeStruct(dec_pool.shape, BF16),
        in_specs=[hbm, vmem, smem],
        out_specs=hbm,
        scratch_shapes=[pltpu.VMEM(dec_pool.shape, BF16), dma((8,)), dma((8,))],
        compiler_params=pltpu.CompilerParams(vmem_limit_bytes=24 * 1024 * 1024),
    )(dec_pool, fresh, dec_lengths)
    return (dec_attn, pre_attn, new_pool, appended)


def solution(mesh):
    in_specs = (
        P("tok", "kv"),
        P("tok", "kv"),
        P(None, "kv"),
        P(None, None, "kv"),
        P("kv"),
        P(None, "kv"),
        P(None, "tok", "kv"),
        P("tok"),
        P("tok"),
        P(None, "tok", "kv"),
        P(),
    )
    out_specs = (P("tok", "kv"), P("tok", "kv"), P(None, "tok", "kv"), P(None, "tok", "kv"))
    return jax.shard_map(
        functools.partial(body, mesh.shape["tok"]),
        mesh=mesh, in_specs=in_specs, out_specs=out_specs, check_vma=False,
    )
```

```python
import functools

import jax
import jax.numpy as jnp
import numpy as np
from jax import lax
from jax.experimental import pallas as pl
from jax.experimental.pallas import tpu as pltpu
from jax.sharding import PartitionSpec as P

HD = 128
THETA = 1000000.0
MESH = pl.DeviceIdType.MESH
CHUNKS = 4
GROUPS = 2
LOG2E = 1.4426950408889634
F32 = jnp.float32
BF16 = jnp.bfloat16


def rotated(value, cosine, sine):
    return value * cosine + pltpu.roll(value, HD // 2, 1) * sine


def dot_nt(a, b):
    return lax.dot_general(a, b, (((1,), (1,)), ((), ())), preferred_element_type=F32)


def step_kernel(
    n_tok,
    dec_x, pre_x, w_q, w_kv, b_q_in, b_kv_in, pool, slots_in, lengths_in, cache, offsets_in,
    rates_in,
    o_dec, o_pre, o_kv, o_new,
    xd, xp, w, raw, kvpool, hist, nk, qs, ms, ls, acc, dq_own, dq_all, dr_send, dr_recv,
    b_q, b_kv, slots, lengths, offsets, rates,
    l_sem, ds_sem, dr_sem, ps_sem, pr_sem, qs_sem, qr_sem, rs_sem, rr_sem,
    cs_sem, cr_sem, ks_sem, kr_sem,
):
    kv = lax.axis_index("kv")
    tok = lax.axis_index("tok")
    mate = tok + 1 - 2 * lax.rem(tok, 2)
    half = lax.rem(tok, 2)
    px = kv + 1 - 2 * lax.rem(kv, 2)
    py = lax.rem(kv + 2, 4)
    pd = lax.rem(px + 2, 4)
    dec_rows, width = dec_x.shape
    pre_rows = pre_x.shape[0]
    q_width = w_q.shape[1]
    heads = q_width // HD
    rows = pre_rows // CHUNKS
    mid = rows // 2
    shard = cache.shape[1]
    scale = HD ** -0.5 * LOG2E

    loads = [
        pltpu.make_async_copy(w_kv, raw, l_sem.at[0]),
        pltpu.make_async_copy(w_q, w.at[:, pl.ds(0, q_width)], l_sem.at[1]),
        pltpu.make_async_copy(dec_x, xd.at[kv], l_sem.at[2]),
        pltpu.make_async_copy(pre_x, xp.at[kv], l_sem.at[3]),
        pltpu.make_async_copy(
            cache, hist.at[:, pl.ds(pl.multiple_of(half * shard, shard), shard)], l_sem.at[4]
        ),
        pltpu.make_async_copy(pool, kvpool, l_sem.at[5]),
        pltpu.make_async_copy(b_q_in, b_q, l_sem.at[6]),
        pltpu.make_async_copy(b_kv_in, b_kv, l_sem.at[7]),
        pltpu.make_async_copy(slots_in, slots, l_sem.at[8]),
        pltpu.make_async_copy(lengths_in, lengths, l_sem.at[9]),
        pltpu.make_async_copy(offsets_in, offsets, l_sem.at[10]),
        pltpu.make_async_copy(rates_in, rates, l_sem.at[11]),
    ]
    for i, load in enumerate(loads):
        if i != 5:
            load.start()

    barrier = pltpu.get_barrier_semaphore()
    for peer in (px, py, pd):
        pl.semaphore_signal(barrier, inc=1, device_id=(peer, tok), device_id_type=MESH)
    for d in range(1, n_tok):
        pl.semaphore_signal(
            barrier, inc=1, device_id=(kv, lax.rem(tok + d, n_tok)), device_id_type=MESH
        )
    pl.semaphore_wait(barrier, n_tok + 2)

    def remote(src, dst, send, recv, where):
        return pltpu.make_async_remote_copy(
            src_ref=src, dst_ref=dst, send_sem=send, recv_sem=recv,
            device_id=where, device_id_type=MESH,
        )

    dec_sends = [
        remote(dec_x, xd.at[kv], ds_sem.at[i], dr_sem.at[i], (peer, tok))
        for i, peer in enumerate((px, py, pd))
    ]
    for send in dec_sends:
        send.start()

    def own_sends(r):
        part = pl.ds(r * rows, rows)
        return [
            remote(pre_x.at[part], xp.at[kv, part], ps_sem.at[r, i], pr_sem.at[r, i], (peer, tok))
            for i, peer in enumerate((px, py))
        ]

    def forwards(r):
        first, second = pl.ds(r * rows, mid), pl.ds(r * rows + mid, mid)
        return [
            remote(xp.at[py, first], xp.at[py, first], ps_sem.at[r, 2], pr_sem.at[r, 2], (px, tok)),
            remote(xp.at[px, second], xp.at[px, second], ps_sem.at[r, 3], pr_sem.at[r, 3], (py, tok)),
        ]

    own = [own_sends(r) for r in range(CHUNKS)]
    onward = [forwards(r) for r in range(CHUNKS)]
    for r in range(2):
        for send in own[r]:
            send.start()
    hist_part = hist.at[:, pl.ds(pl.multiple_of(half * shard, shard), shard)]
    cache_send = remote(cache, hist_part, cs_sem, cr_sem, (kv, mate))
    cache_send.start()

    def pump(r):
        for send in own[r]:
            send.wait_recv()
        for send in onward[r]:
            send.start()
        if r + 2 < CHUNKS:
            for send in own[r + 2]:
                send.start()

    loads[0].wait()
    block, beside = 256, 8
    row = lax.broadcasted_iota(jnp.int32, (block, block), 0)
    col = lax.broadcasted_iota(jnp.int32, (block, block), 1)
    wanted = jnp.where(row < block // 2, 2 * row, 2 * row - block + 1)
    permute = jnp.where(col == wanted, 1.0, 0.0).astype(BF16)

    def part_weights(i, carry):
        tiles = jnp.concatenate(
            [raw[pl.ds(pl.multiple_of((i * beside + j) * block, block), block), :]
             for j in range(beside)],
            axis=1,
        )
        parted = jnp.dot(permute, tiles, preferred_element_type=F32).astype(BF16)
        for j in range(beside):
            half_block = block // 2
            where = pl.ds(pl.multiple_of((i * beside + j) * half_block, half_block), half_block)
            w[where, pl.ds(q_width, HD)] = parted[:half_block, j * HD:(j + 1) * HD]
            w[where, pl.ds(q_width + HD, HD)] = parted[half_block:, j * HD:(j + 1) * HD]
        return carry

    lax.fori_loop(0, raw.shape[0] // (block * beside), part_weights, 0)
    pump(0)
    for load in loads[6:]:
        load.wait()

    def project(x_ref, start, amount):
        def add(s, total):
            return total + jnp.dot(
                x_ref[s, pl.ds(start, amount), :],
                w[pl.ds(pl.multiple_of(s * width, width), width), :],
                preferred_element_type=F32,
            )

        total = lax.fori_loop(0, 4, add, jnp.zeros((amount, q_width + 2 * HD), F32))
        bias = jnp.concatenate([b_q[...].reshape(1, q_width), b_kv[0:1, :], b_kv[1:2, :]], axis=1)
        return total + bias

    loads[1].wait()
    loads[5].start()
    loads[2].wait()
    for send in dec_sends:
        send.wait_recv()
    dq_own[...] = project(xd, 0, dec_rows).astype(BF16)
    q_sends = [
        remote(dq_own, dq_all.at[tok], qs_sem.at[d - 1], qr_sem.at[d - 1],
               (kv, lax.rem(tok + d, n_tok)))
        for d in range(1, n_tok)
    ]
    for send in q_sends:
        send.start()
    dq_all[tok] = dq_own[...]

    pump(1)
    pump(2)

    for send in q_sends:
        send.wait_recv()
    requests = n_tok * dec_rows
    row = lax.broadcasted_iota(jnp.int32, (dec_rows, requests), 0)
    col = lax.broadcasted_iota(jnp.int32, (dec_rows, requests), 1)
    row_t = lax.broadcasted_iota(jnp.int32, (requests, dec_rows), 0)
    col_t = lax.broadcasted_iota(jnp.int32, (requests, dec_rows), 1)
    stacked = heads * dec_rows
    slot_of = lax.rem(lax.broadcasted_iota(jnp.int32, (stacked, 1), 0), dec_rows)
    line = lax.broadcasted_iota(jnp.int32, (dec_rows, HD), 0)
    chosen = jnp.zeros((dec_rows, requests), F32)
    chosen_t = jnp.zeros((requests, dec_rows), F32)
    first = jnp.zeros((stacked, 1), jnp.int32)
    last = jnp.zeros((stacked, 1), jnp.int32)
    places = jnp.zeros((dec_rows, HD), jnp.int32)
    begin = jnp.int32(0)
    for s in range(dec_rows):
        request = slots[s]
        length = lengths[s]
        chosen = jnp.where((row == s) & (col == request), 1.0, chosen)
        chosen_t = jnp.where((col_t == s) & (row_t == request), 1.0, chosen_t)
        first = jnp.where(slot_of == s, begin, first)
        last = jnp.where(slot_of == s, begin + length, last)
        places = jnp.where(line == s, length, places)
        begin = begin + length + 1
    chosen = chosen.astype(BF16)
    chosen_t = chosen_t.astype(BF16)
    every = dq_all[...].reshape(requests, q_width + 2 * HD)
    mine = jnp.dot(chosen, every, preferred_element_type=F32)
    lane = lax.broadcasted_iota(jnp.int32, (1, HD), 1)
    sign = jnp.where(lane < HD // 2, -1.0, 1.0)
    angles = places.astype(F32) * rates[...]
    cosine = jnp.cos(angles)
    sine = jnp.sin(angles) * sign
    turned = jnp.concatenate(
        [rotated(mine[:, h * HD:(h + 1) * HD], cosine, sine) for h in range(heads)], axis=0
    ).astype(BF16)
    fresh_k = rotated(mine[:, q_width:q_width + HD], cosine, sine).astype(BF16)
    fresh_v = mine[:, q_width + HD:].astype(BF16)
    o_new[0] = fresh_k
    o_new[1] = fresh_v
    same = slot_of == lax.broadcasted_iota(jnp.int32, (stacked, dec_rows), 1)
    scores = jnp.where(same, dot_nt(turned, fresh_k) * scale, -jnp.inf)
    peak = jnp.max(scores, axis=1, keepdims=True)
    powers = jnp.exp2(scores - peak)
    total = jnp.sum(powers, axis=1, keepdims=True)
    mixed = jnp.dot(powers.astype(BF16), fresh_v, preferred_element_type=F32)
    loads[5].wait()
    tile = 2048

    def visit(t, carry):
        peak, total, mixed = carry
        where = pl.ds(pl.multiple_of(t * tile, tile), tile)
        spots = t * tile + lax.broadcasted_iota(jnp.int32, (stacked, tile), 1)
        scores = dot_nt(turned, kvpool[0, where, :]) * scale
        scores = jnp.where((spots >= first) & (spots < last), scores, -jnp.inf)
        top = jnp.maximum(peak, jnp.max(scores, axis=1, keepdims=True))
        powers = jnp.exp2(scores - top)
        fade = jnp.exp2(peak - top)
        total = total * fade + jnp.sum(powers, axis=1, keepdims=True)
        mixed = mixed * fade + jnp.dot(
            powers.astype(BF16), kvpool[1, where, :], preferred_element_type=F32
        )
        return top, total, mixed

    peak, total, mixed = lax.fori_loop(0, pool.shape[1] // tile, visit, (peak, total, mixed))
    result = (mixed / total).astype(BF16)
    result = jnp.concatenate(
        [result[h * dec_rows:(h + 1) * dec_rows] for h in range(heads)], axis=1
    )
    spread = jnp.dot(chosen_t, result, preferred_element_type=F32).astype(BF16)
    dr_send[...] = spread.reshape(n_tok, dec_rows, q_width)
    r_sends = []
    for d in range(1, n_tok):
        peer = lax.rem(tok + d, n_tok)
        r_sends.append(
            remote(dr_send.at[peer], dr_recv.at[tok], rs_sem.at[d - 1], rr_sem.at[d - 1],
                   (kv, peer))
        )
    for send in r_sends:
        send.start()
    dr_recv[tok] = dr_send[tok]
    pump(3)

    offset = offsets[lax.div(tok, 2)]
    loads[3].wait()
    loads[4].wait()
    cache_send.wait_recv()
    key_sends = []
    rows = pre_rows // GROUPS
    for r in range(GROUPS):
        for piece in range(r * CHUNKS // GROUPS, (r + 1) * CHUNKS // GROUPS):
            for send in onward[piece]:
                send.wait_recv()
        value = project(xp, r * rows, rows)
        place = pl.multiple_of(half * pre_rows + r * rows, rows)
        positions = offset + place + lax.broadcasted_iota(jnp.int32, (rows, HD), 0)
        angles = positions.astype(F32) * rates[...]
        cosine = jnp.cos(angles)
        sine = jnp.sin(angles) * sign
        queries = jnp.concatenate(
            [rotated(value[:, h * HD:(h + 1) * HD], cosine, sine) for h in range(heads)], axis=0
        ).astype(BF16)
        qs[r] = queries
        new_k = rotated(value[:, q_width:q_width + HD], cosine, sine).astype(BF16)
        new_v = value[:, q_width + HD:].astype(BF16)
        o_kv[0, pl.ds(r * rows, rows), :] = new_k
        o_kv[1, pl.ds(r * rows, rows), :] = new_v
        nk[0, pl.ds(place, rows), :] = new_k
        nk[1, pl.ds(place, rows), :] = new_v
        part = nk.at[:, pl.ds(place, rows)]
        send = remote(part, part, ks_sem.at[r], kr_sem.at[r], (kv, mate))
        send.start()
        key_sends.append(send)
        scores = dot_nt(queries, hist[0]) * scale
        cached = lax.broadcasted_iota(jnp.int32, (1, 2 * shard), 1) < offset
        scores = jnp.where(cached, scores, -jnp.inf)
        peak = jnp.max(scores, axis=1, keepdims=True)
        powers = jnp.exp2(scores - peak)
        total = jnp.sum(powers, axis=1, keepdims=True)
        acc[r] = jnp.dot(powers.astype(BF16), hist[1], preferred_element_type=F32)
        ms[r] = jnp.broadcast_to(peak, (heads * rows, HD))
        ls[r] = jnp.broadcast_to(total, (heads * rows, HD))

    for send in r_sends:
        send.wait_recv()
    gathered = dr_recv[0].astype(F32)
    for o in range(1, n_tok):
        gathered = gathered + dr_recv[o].astype(F32)
    o_dec[...] = gathered.astype(BF16)

    for send in key_sends:
        send.wait_recv()
    inner = lax.rem(lax.broadcasted_iota(jnp.int32, (heads * rows, 1), 0), rows)
    later = lax.broadcasted_iota(jnp.int32, (heads * rows, 2 * pre_rows), 1)

    def finish(r, carry):
        scores = dot_nt(qs[r], nk[0]) * scale
        scores = jnp.where(later <= inner + (half * pre_rows + r * rows), scores, -jnp.inf)
        peak = ms[r][:, :1]
        top = jnp.maximum(peak, jnp.max(scores, axis=1, keepdims=True))
        powers = jnp.exp2(scores - top)
        fade = jnp.exp2(peak - top)
        total = ls[r][:, :1] * fade + jnp.sum(powers, axis=1, keepdims=True)
        mixed = acc[r] * fade + jnp.dot(powers.astype(BF16), nk[1], preferred_element_type=F32)
        result = (mixed / total).astype(BF16)
        for h in range(heads):
            o_pre[pl.ds(pl.multiple_of(r * rows, rows), rows), h * HD:(h + 1) * HD] = (
                result[h * rows:(h + 1) * rows]
            )
        return carry

    lax.fori_loop(0, GROUPS, finish, 0)

    for send in dec_sends + q_sends + r_sends + key_sends + [cache_send]:
        send.wait_send()
    for r in range(CHUNKS):
        for send in own[r] + onward[r]:
            send.wait_send()


def pool_kernel(
    pool, fresh_in, lengths_in, dec_in, pre_in, kv_in, out, dec_out, pre_out, kv_out,
    buffer, fresh, lengths, dec_b, pre_b, kv_b, in_sem, out_sem,
):
    parts = 4
    size = pool.shape[1] // parts
    pieces = [(c, pl.ds(i * size, size)) for c in range(2) for i in range(parts)]
    reads = [
        pltpu.make_async_copy(pool.at[c, p], buffer.at[c, p], in_sem.at[i])
        for i, (c, p) in enumerate(pieces)
    ]
    writes = [
        pltpu.make_async_copy(buffer.at[c, p], out.at[c, p], out_sem.at[i])
        for i, (c, p) in enumerate(pieces)
    ]
    count = len(pieces)
    rest = ((dec_in, dec_b, dec_out), (pre_in, pre_b, pre_out), (kv_in, kv_b, kv_out))
    for i, (source, held, target) in enumerate(rest):
        reads.append(pltpu.make_async_copy(source, held, in_sem.at[count + i]))
        writes.append(pltpu.make_async_copy(held, target, out_sem.at[count + i]))
    reads.append(pltpu.make_async_copy(fresh_in, fresh, in_sem.at[count + 3]))
    reads.append(pltpu.make_async_copy(lengths_in, lengths, in_sem.at[count + 4]))
    for copy in reads:
        copy.start()
    for copy in reads:
        copy.wait()
    line = lax.broadcasted_iota(jnp.int32, (16, HD), 0)
    end = jnp.int32(0)
    for s in range(fresh.shape[1]):
        end = end + lengths[s]
        base = pl.multiple_of(lax.div(end, 16) * 16, 16)
        for c in range(2):
            new_row = fresh[c, s:s + 1, :].astype(F32)
            held = buffer[c, pl.ds(base, 16), :].astype(F32)
            buffer[c, pl.ds(base, 16), :] = jnp.where(
                line == end - base, new_row, held
            ).astype(BF16)
        end = end + 1
    for copy in writes:
        copy.start()
    for copy in writes:
        copy.wait()


def body(
    n_tok, dec_tokens, pre_tokens, w_query, w_keyval, b_query, b_keyval,
    dec_pool, owner_slots, dec_lengths, pre_cache, pre_offsets,
):
    dec_rows, width = dec_tokens.shape
    pre_rows = pre_tokens.shape[0]
    q_width = w_query.shape[1]
    heads = q_width // HD
    depth = w_query.shape[0]
    out_width = q_width + 2 * HD
    rows = pre_rows // GROUPS
    shard = pre_cache.shape[1]
    spread = np.arange(HD // 2, dtype=np.float32) * np.float32(2.0 / HD)
    rates = np.power(np.float32(THETA), -spread).astype(np.float32)
    rates = jnp.asarray(np.concatenate([rates, rates])[None, :])
    hbm = pl.BlockSpec(memory_space=pl.ANY)
    vmem = pl.BlockSpec(memory_space=pltpu.VMEM)
    dma = pltpu.SemaphoreType.DMA
    dec_attn, pre_attn, appended, fresh = pl.pallas_call(
        functools.partial(step_kernel, n_tok),
        name="attention_step",
        out_shape=(
            jax.ShapeDtypeStruct((dec_rows, q_width), BF16),
            jax.ShapeDtypeStruct((pre_rows, q_width), BF16),
            jax.ShapeDtypeStruct((2, pre_rows, HD), BF16),
            jax.ShapeDtypeStruct((2, dec_rows, HD), BF16),
        ),
        in_specs=[hbm] * 12,
        out_specs=(vmem, vmem, vmem, vmem),
        scratch_shapes=[
            pltpu.VMEM((4, dec_rows, width), BF16),
            pltpu.VMEM((4, pre_rows, width), BF16),
            pltpu.VMEM((depth, out_width), BF16),
            pltpu.VMEM((2 * depth, HD), BF16),
            pltpu.VMEM(dec_pool.shape, BF16),
            pltpu.VMEM((2, 2 * shard, HD), BF16),
            pltpu.VMEM((2, 2 * pre_rows, HD), BF16),
            pltpu.VMEM((GROUPS, heads * rows, HD), BF16),
            pltpu.VMEM((GROUPS, heads * rows, HD), F32),
            pltpu.VMEM((GROUPS, heads * rows, HD), F32),
            pltpu.VMEM((GROUPS, heads * rows, HD), F32),
            pltpu.VMEM((dec_rows, out_width), BF16),
            pltpu.VMEM((n_tok, dec_rows, out_width), BF16),
            pltpu.VMEM((n_tok, dec_rows, q_width), BF16),
            pltpu.VMEM((n_tok, dec_rows, q_width), BF16),
            pltpu.VMEM((q_width,), F32),
            pltpu.VMEM((2, HD), F32),
            pltpu.SMEM(owner_slots.shape, jnp.int32),
            pltpu.SMEM(dec_lengths.shape, jnp.int32),
            pltpu.SMEM(pre_offsets.shape, jnp.int32),
            pltpu.VMEM((1, HD), F32),
            dma((12,)),
            dma((3,)), dma((3,)),
            dma((CHUNKS, 4)), dma((CHUNKS, 4)),
            dma((n_tok - 1,)), dma((n_tok - 1,)),
            dma((n_tok - 1,)), dma((n_tok - 1,)),
            dma, dma,
            dma((GROUPS,)), dma((GROUPS,)),
        ],
        compiler_params=pltpu.CompilerParams(
            collective_id=0, has_side_effects=True, vmem_limit_bytes=64 * 1024 * 1024
        ),
    )(
        dec_tokens, pre_tokens, w_query, w_keyval.reshape(2 * depth, HD),
        b_query, b_keyval, dec_pool, owner_slots, dec_lengths,
        pre_cache, pre_offsets, rates,
    )
    rest = (dec_attn, pre_attn, appended)
    new_pool, dec_attn, pre_attn, appended = pl.pallas_call(
        pool_kernel,
        name="append_rows",
        out_shape=(
            jax.ShapeDtypeStruct(dec_pool.shape, BF16),
            *(jax.ShapeDtypeStruct(value.shape, BF16) for value in rest),
        ),
        in_specs=[hbm] * 6,
        out_specs=[hbm] * 4,
        scratch_shapes=[
            pltpu.VMEM(dec_pool.shape, BF16),
            pltpu.VMEM(fresh.shape, BF16),
            pltpu.SMEM(dec_lengths.shape, jnp.int32),
            *(pltpu.VMEM(value.shape, BF16) for value in rest),
            dma((13,)), dma((11,)),
        ],
        compiler_params=pltpu.CompilerParams(vmem_limit_bytes=64 * 1024 * 1024),
    )(dec_pool, fresh, dec_lengths, *rest)
    return (dec_attn, pre_attn, new_pool, appended)


def solution(mesh):
    in_specs = (
        P("tok", "kv"),
        P("tok", "kv"),
        P(None, "kv"),
        P(None, None, "kv"),
        P("kv"),
        P(None, "kv"),
        P(None, "tok", "kv"),
        P("tok"),
        P("tok"),
        P(None, "tok", "kv"),
        P(),
    )
    out_specs = (P("tok", "kv"), P("tok", "kv"), P(None, "tok", "kv"), P(None, "tok", "kv"))
    return jax.shard_map(
        functools.partial(body, mesh.shape["tok"]),
        mesh=mesh, in_specs=in_specs, out_specs=out_specs, check_vma=False,
    )
```

```python
import functools

import jax
import jax.numpy as jnp
import numpy as np
from jax import lax
from jax.experimental import pallas as pl
from jax.experimental.pallas import tpu as pltpu
from jax.sharding import PartitionSpec as P

HD = 128
THETA = 1000000.0
MESH = pl.DeviceIdType.MESH
CHUNKS = 4
GROUPS = 2
LOG2E = 1.4426950408889634
F32 = jnp.float32
BF16 = jnp.bfloat16


def rotated(value, cosine, sine):
    return value * cosine + pltpu.roll(value, HD // 2, 1) * sine


def dot_nt(a, b):
    return lax.dot_general(a, b, (((1,), (1,)), ((), ())), preferred_element_type=F32)


def lane_max(run, value):
    for j in range(value.shape[1] // HD):
        run = jnp.maximum(run, value[:, j * HD:(j + 1) * HD])
    return run


def lane_sum(run, value):
    for j in range(value.shape[1] // HD):
        run = run + value[:, j * HD:(j + 1) * HD]
    return run


def step_kernel(
    n_tok,
    dec_x, pre_x, w_q, w_kv, b_q_in, b_kv_in, pool, slots_in, lengths_in, cache, offsets_in,
    rates_in,
    o_dec, o_pre, o_kv, o_new,
    xd, xp, w, raw, kvpool, hist, nk, qs, ms, ls, acc, dq_own, dq_all, dr_send, dr_recv,
    b_q, b_kv, slots, lengths, offsets, rates, marks, long_marks,
    l_sem, ds_sem, dr_sem, ps_sem, pr_sem, qs_sem, qr_sem, rs_sem, rr_sem,
    cs_sem, cr_sem, ks_sem, kr_sem,
):
    kv = lax.axis_index("kv")
    tok = lax.axis_index("tok")
    mate = tok + 1 - 2 * lax.rem(tok, 2)
    half = lax.rem(tok, 2)
    px = kv + 1 - 2 * lax.rem(kv, 2)
    py = lax.rem(kv + 2, 4)
    pd = lax.rem(px + 2, 4)
    dec_rows, width = dec_x.shape
    pre_rows = pre_x.shape[0]
    q_width = w_q.shape[1]
    heads = q_width // HD
    rows = pre_rows // CHUNKS
    mid = rows // 2
    shard = cache.shape[1]
    scale = HD ** -0.5 * LOG2E

    loads = [
        pltpu.make_async_copy(w_kv, raw, l_sem.at[0]),
        pltpu.make_async_copy(w_q, w.at[:, pl.ds(0, q_width)], l_sem.at[1]),
        pltpu.make_async_copy(dec_x, xd.at[kv], l_sem.at[2]),
        pltpu.make_async_copy(pre_x, xp.at[kv], l_sem.at[3]),
        pltpu.make_async_copy(
            cache, hist.at[:, pl.ds(pl.multiple_of(half * shard, shard), shard)], l_sem.at[4]
        ),
        pltpu.make_async_copy(pool, kvpool, l_sem.at[5]),
        pltpu.make_async_copy(b_q_in, b_q, l_sem.at[6]),
        pltpu.make_async_copy(b_kv_in, b_kv, l_sem.at[7]),
        pltpu.make_async_copy(slots_in, slots, l_sem.at[8]),
        pltpu.make_async_copy(lengths_in, lengths, l_sem.at[9]),
        pltpu.make_async_copy(offsets_in, offsets, l_sem.at[10]),
        pltpu.make_async_copy(rates_in, rates, l_sem.at[11]),
    ]
    for i, load in enumerate(loads):
        if i != 5:
            load.start()

    barrier = pltpu.get_barrier_semaphore()
    for peer in (px, py, pd):
        pl.semaphore_signal(barrier, inc=1, device_id=(peer, tok), device_id_type=MESH)
    for d in range(1, n_tok):
        pl.semaphore_signal(
            barrier, inc=1, device_id=(kv, lax.rem(tok + d, n_tok)), device_id_type=MESH
        )
    pl.semaphore_wait(barrier, n_tok + 2)

    def remote(src, dst, send, recv, where):
        return pltpu.make_async_remote_copy(
            src_ref=src, dst_ref=dst, send_sem=send, recv_sem=recv,
            device_id=where, device_id_type=MESH,
        )

    dec_sends = [
        remote(dec_x, xd.at[kv], ds_sem.at[i], dr_sem.at[i], (peer, tok))
        for i, peer in enumerate((px, py, pd))
    ]
    for send in dec_sends:
        send.start()

    def own_sends(r):
        part = pl.ds(r * rows, rows)
        return [
            remote(pre_x.at[part], xp.at[kv, part], ps_sem.at[r, i], pr_sem.at[r, i], (peer, tok))
            for i, peer in enumerate((px, py))
        ]

    def forwards(r):
        first, second = pl.ds(r * rows, mid), pl.ds(r * rows + mid, mid)
        return [
            remote(xp.at[py, first], xp.at[py, first], ps_sem.at[r, 2], pr_sem.at[r, 2], (px, tok)),
            remote(xp.at[px, second], xp.at[px, second], ps_sem.at[r, 3], pr_sem.at[r, 3], (py, tok)),
        ]

    own = [own_sends(r) for r in range(CHUNKS)]
    onward = [forwards(r) for r in range(CHUNKS)]
    for r in range(2):
        for send in own[r]:
            send.start()
    hist_part = hist.at[:, pl.ds(pl.multiple_of(half * shard, shard), shard)]
    cache_send = remote(cache, hist_part, cs_sem, cr_sem, (kv, mate))
    cache_send.start()

    def pump(r):
        for send in own[r]:
            send.wait_recv()
        for send in onward[r]:
            send.start()
        if r + 2 < CHUNKS:
            for send in own[r + 2]:
                send.start()

    loads[0].wait()
    block, beside = 256, 8
    row = lax.broadcasted_iota(jnp.int32, (block, block), 0)
    col = lax.broadcasted_iota(jnp.int32, (block, block), 1)
    wanted = jnp.where(row < block // 2, 2 * row, 2 * row - block + 1)
    permute = jnp.where(col == wanted, 1.0, 0.0).astype(BF16)

    def part_weights(i, carry):
        tiles = jnp.concatenate(
            [raw[pl.ds(pl.multiple_of((i * beside + j) * block, block), block), :]
             for j in range(beside)],
            axis=1,
        )
        parted = jnp.dot(permute, tiles, preferred_element_type=F32).astype(BF16)
        for j in range(beside):
            half_block = block // 2
            where = pl.ds(pl.multiple_of((i * beside + j) * half_block, half_block), half_block)
            w[where, pl.ds(q_width, HD)] = parted[:half_block, j * HD:(j + 1) * HD]
            w[where, pl.ds(q_width + HD, HD)] = parted[half_block:, j * HD:(j + 1) * HD]
        return carry

    lax.fori_loop(0, raw.shape[0] // (block * beside), part_weights, 0)
    pump(0)
    for load in loads[6:]:
        load.wait()

    def project(x_ref, start, amount, arrive):
        total = jnp.concatenate([b_q[...].reshape(1, q_width), b_kv[0:1, :], b_kv[1:2, :]], axis=1)
        for source in (kv, px, py, pd):
            if source is pd:
                arrive()
            total = total + jnp.dot(
                x_ref[source, pl.ds(start, amount), :],
                w[pl.ds(pl.multiple_of(source * width, width), width), :],
                preferred_element_type=F32,
            )
        return total

    loads[1].wait()
    loads[5].start()
    loads[2].wait()
    for send in dec_sends:
        send.wait_recv()
    dq_own[...] = project(xd, 0, dec_rows, lambda: None).astype(BF16)
    q_sends = [
        remote(dq_own, dq_all.at[tok], qs_sem.at[d - 1], qr_sem.at[d - 1],
               (kv, lax.rem(tok + d, n_tok)))
        for d in range(1, n_tok)
    ]
    for send in q_sends:
        send.start()
    dq_all[tok] = dq_own[...]

    pump(1)
    pump(2)

    for send in q_sends:
        send.wait_recv()
    requests = n_tok * dec_rows
    row = lax.broadcasted_iota(jnp.int32, (dec_rows, requests), 0)
    col = lax.broadcasted_iota(jnp.int32, (dec_rows, requests), 1)
    row_t = lax.broadcasted_iota(jnp.int32, (requests, dec_rows), 0)
    col_t = lax.broadcasted_iota(jnp.int32, (requests, dec_rows), 1)
    stacked = heads * dec_rows
    slot_of = lax.rem(lax.broadcasted_iota(jnp.int32, (stacked, 1), 0), dec_rows)
    line = lax.broadcasted_iota(jnp.int32, (dec_rows, HD), 0)
    chosen = jnp.zeros((dec_rows, requests), F32)
    chosen_t = jnp.zeros((requests, dec_rows), F32)
    first = jnp.zeros((stacked, 1), jnp.int32)
    last = jnp.zeros((stacked, 1), jnp.int32)
    places = jnp.zeros((dec_rows, HD), jnp.int32)
    begin = jnp.int32(0)
    for s in range(dec_rows):
        request = slots[s]
        length = lengths[s]
        chosen = jnp.where((row == s) & (col == request), 1.0, chosen)
        chosen_t = jnp.where((col_t == s) & (row_t == request), 1.0, chosen_t)
        first = jnp.where(slot_of == s, begin, first)
        last = jnp.where(slot_of == s, begin + length, last)
        places = jnp.where(line == s, length, places)
        begin = begin + length + 1
    chosen = chosen.astype(BF16)
    chosen_t = chosen_t.astype(BF16)
    every = dq_all[...].reshape(requests, q_width + 2 * HD)
    mine = jnp.dot(chosen, every, preferred_element_type=F32)
    lane = lax.broadcasted_iota(jnp.int32, (1, HD), 1)
    sign = jnp.where(lane < HD // 2, -1.0, 1.0)
    angles = places.astype(F32) * rates[...]
    cosine = jnp.cos(angles)
    sine = jnp.sin(angles) * sign
    turned = jnp.concatenate(
        [rotated(mine[:, h * HD:(h + 1) * HD], cosine, sine) for h in range(heads)], axis=0
    ).astype(BF16)
    fresh_k = rotated(mine[:, q_width:q_width + HD], cosine, sine).astype(BF16)
    fresh_v = mine[:, q_width + HD:].astype(BF16)
    o_new[0] = fresh_k
    o_new[1] = fresh_v
    same = slot_of == lax.broadcasted_iota(jnp.int32, (stacked, dec_rows), 1)
    scores = jnp.where(same, dot_nt(turned, fresh_k) * scale, -jnp.inf)
    peak = jnp.max(scores, axis=1, keepdims=True)
    powers = jnp.exp2(scores - peak)
    total = jnp.sum(powers, axis=1, keepdims=True)
    mixed = jnp.dot(powers.astype(BF16), fresh_v, preferred_element_type=F32)
    loads[5].wait()
    wide, tile = 2048, 512
    strides = pool.shape[1] // wide

    def score(t, run):
        for j in range(wide // tile):
            start = pl.multiple_of(t * wide + j * tile, tile)
            spots = start + lax.broadcasted_iota(jnp.int32, (stacked, tile), 1)
            value = dot_nt(turned, kvpool[0, pl.ds(start, tile), :]) * scale
            value = jnp.where((spots >= first) & (spots < last), value, -jnp.inf)
            long_marks[:, pl.ds(start, tile)] = value
            run = lane_max(run, value)
        return run

    run = lax.fori_loop(0, strides, score, jnp.broadcast_to(peak, (stacked, HD)))
    top = jnp.max(run, axis=1, keepdims=True)
    fade = jnp.exp2(peak - top)

    def mix(t, carry):
        sums, mixed = carry
        for j in range(wide // tile):
            start = pl.multiple_of(t * wide + j * tile, tile)
            powers = jnp.exp2(long_marks[:, pl.ds(start, tile)] - top)
            sums = lane_sum(sums, powers)
            mixed = mixed + jnp.dot(
                powers.astype(BF16), kvpool[1, pl.ds(start, tile), :], preferred_element_type=F32
            )
        return sums, mixed

    sums, mixed = lax.fori_loop(
        0, strides, mix, (jnp.zeros((stacked, HD), F32), mixed * fade)
    )
    total = total * fade + jnp.sum(sums, axis=1, keepdims=True)
    result = (mixed / total).astype(BF16)
    result = jnp.concatenate(
        [result[h * dec_rows:(h + 1) * dec_rows] for h in range(heads)], axis=1
    )
    spread = jnp.dot(chosen_t, result, preferred_element_type=F32).astype(BF16)
    dr_send[...] = spread.reshape(n_tok, dec_rows, q_width)
    r_sends = []
    for d in range(1, n_tok):
        peer = lax.rem(tok + d, n_tok)
        r_sends.append(
            remote(dr_send.at[peer], dr_recv.at[tok], rs_sem.at[d - 1], rr_sem.at[d - 1],
                   (kv, peer))
        )
    for send in r_sends:
        send.start()
    dr_recv[tok] = dr_send[tok]
    pump(3)

    offset = offsets[lax.div(tok, 2)]
    loads[3].wait()
    loads[4].wait()
    cache_send.wait_recv()
    key_sends = []
    rows = pre_rows // GROUPS
    span = 256
    for r in range(GROUPS):

        def arrive():
            for piece in range(r * CHUNKS // GROUPS, (r + 1) * CHUNKS // GROUPS):
                for send in onward[piece]:
                    send.wait_recv()

        value = project(xp, r * rows, rows, arrive)
        place = pl.multiple_of(half * pre_rows + r * rows, rows)
        positions = offset + place + lax.broadcasted_iota(jnp.int32, (rows, HD), 0)
        angles = positions.astype(F32) * rates[...]
        cosine = jnp.cos(angles)
        sine = jnp.sin(angles) * sign
        queries = jnp.concatenate(
            [rotated(value[:, h * HD:(h + 1) * HD], cosine, sine) for h in range(heads)], axis=0
        ).astype(BF16)
        qs[r] = queries
        new_k = rotated(value[:, q_width:q_width + HD], cosine, sine).astype(BF16)
        new_v = value[:, q_width + HD:].astype(BF16)
        o_kv[0, pl.ds(r * rows, rows), :] = new_k
        o_kv[1, pl.ds(r * rows, rows), :] = new_v
        nk[0, pl.ds(place, rows), :] = new_k
        nk[1, pl.ds(place, rows), :] = new_v
        part = nk.at[:, pl.ds(place, rows)]
        send = remote(part, part, ks_sem.at[r], kr_sem.at[r], (kv, mate))
        send.start()
        key_sends.append(send)

        def cached_head(h, carry):
            where = pl.ds(pl.multiple_of(h * rows, rows), rows)
            query = qs[r, where, :]
            run = jnp.full((rows, HD), -jnp.inf, F32)
            for t in range(2 * shard // span):
                cached = lax.broadcasted_iota(jnp.int32, (1, span), 1) + t * span < offset
                value = dot_nt(query, hist[0, t * span:(t + 1) * span, :]) * scale
                value = jnp.where(cached, value, -jnp.inf)
                marks[:, t * span:(t + 1) * span] = value
                run = lane_max(run, value)
            top = jnp.max(run, axis=1, keepdims=True)
            sums = jnp.zeros((rows, HD), F32)
            mixed = jnp.zeros((rows, HD), F32)
            for t in range(2 * shard // span):
                powers = jnp.exp2(marks[:, t * span:(t + 1) * span] - top)
                sums = lane_sum(sums, powers)
                mixed = mixed + jnp.dot(
                    powers.astype(BF16), hist[1, t * span:(t + 1) * span, :],
                    preferred_element_type=F32,
                )
            acc[r, where, :] = mixed
            ms[r, where, :] = jnp.broadcast_to(top, (rows, HD))
            ls[r, where, :] = jnp.broadcast_to(jnp.sum(sums, axis=1, keepdims=True), (rows, HD))
            return carry

        lax.fori_loop(0, heads, cached_head, 0)

    for send in r_sends:
        send.wait_recv()
    gathered = dr_recv[0].astype(F32)
    for o in range(1, n_tok):
        gathered = gathered + dr_recv[o].astype(F32)
    o_dec[...] = gathered.astype(BF16)

    for send in key_sends:
        send.wait_recv()
    inner = lax.broadcasted_iota(jnp.int32, (rows, span), 0)
    later = lax.broadcasted_iota(jnp.int32, (rows, span), 1)

    for r in range(GROUPS):
        for h in range(heads):
            part = slice(h * rows, (h + 1) * rows)
            query = qs[r, part, :]
            peak = ms[r, part, :]
            run = peak
            values = []
            for t in range(2 * pre_rows // span):
                value = dot_nt(query, nk[0, t * span:(t + 1) * span, :]) * scale
                allowed = later + t * span <= inner + (half * pre_rows + r * rows)
                value = jnp.where(allowed, value, -jnp.inf)
                values.append(value)
                run = lane_max(run, value)
            top = jnp.max(run, axis=1, keepdims=True)
            fade = jnp.exp2(peak - top)
            mixed = acc[r, part, :] * fade
            sums = jnp.zeros((rows, HD), F32)
            for t, value in enumerate(values):
                powers = jnp.exp2(value - top)
                sums = lane_sum(sums, powers)
                mixed = mixed + jnp.dot(
                    powers.astype(BF16), nk[1, t * span:(t + 1) * span, :],
                    preferred_element_type=F32,
                )
            total = ls[r, part, :] * fade + jnp.sum(sums, axis=1, keepdims=True)
            o_pre[r * rows:(r + 1) * rows, h * HD:(h + 1) * HD] = (mixed / total).astype(BF16)

    for send in dec_sends + q_sends + r_sends + key_sends + [cache_send]:
        send.wait_send()
    for r in range(CHUNKS):
        for send in own[r] + onward[r]:
            send.wait_send()


def pool_kernel(
    pool, fresh_in, lengths_in, dec_in, pre_in, kv_in, out, dec_out, pre_out, kv_out,
    buffer, fresh, lengths, dec_b, pre_b, kv_b, in_sem, out_sem,
):
    parts = 4
    size = pool.shape[1] // parts
    pieces = [(c, pl.ds(i * size, size)) for c in range(2) for i in range(parts)]
    reads = [
        pltpu.make_async_copy(pool.at[c, p], buffer.at[c, p], in_sem.at[i])
        for i, (c, p) in enumerate(pieces)
    ]
    writes = [
        pltpu.make_async_copy(buffer.at[c, p], out.at[c, p], out_sem.at[i])
        for i, (c, p) in enumerate(pieces)
    ]
    count = len(pieces)
    rest = ((dec_in, dec_b, dec_out), (pre_in, pre_b, pre_out), (kv_in, kv_b, kv_out))
    for i, (source, held, target) in enumerate(rest):
        reads.append(pltpu.make_async_copy(source, held, in_sem.at[count + i]))
        writes.append(pltpu.make_async_copy(held, target, out_sem.at[count + i]))
    reads.append(pltpu.make_async_copy(fresh_in, fresh, in_sem.at[count + 3]))
    reads.append(pltpu.make_async_copy(lengths_in, lengths, in_sem.at[count + 4]))
    for copy in reads:
        copy.start()
    for copy in reads:
        copy.wait()
    line = lax.broadcasted_iota(jnp.int32, (16, HD), 0)
    end = jnp.int32(0)
    for s in range(fresh.shape[1]):
        end = end + lengths[s]
        base = pl.multiple_of(lax.div(end, 16) * 16, 16)
        for c in range(2):
            new_row = fresh[c, s:s + 1, :].astype(F32)
            held = buffer[c, pl.ds(base, 16), :].astype(F32)
            buffer[c, pl.ds(base, 16), :] = jnp.where(
                line == end - base, new_row, held
            ).astype(BF16)
        end = end + 1
    for copy in writes:
        copy.start()
    for copy in writes:
        copy.wait()


def body(
    n_tok, dec_tokens, pre_tokens, w_query, w_keyval, b_query, b_keyval,
    dec_pool, owner_slots, dec_lengths, pre_cache, pre_offsets,
):
    dec_rows, width = dec_tokens.shape
    pre_rows = pre_tokens.shape[0]
    q_width = w_query.shape[1]
    heads = q_width // HD
    depth = w_query.shape[0]
    out_width = q_width + 2 * HD
    rows = pre_rows // GROUPS
    shard = pre_cache.shape[1]
    spread = np.arange(HD // 2, dtype=np.float32) * np.float32(2.0 / HD)
    rates = np.power(np.float32(THETA), -spread).astype(np.float32)
    rates = jnp.asarray(np.concatenate([rates, rates])[None, :])
    hbm = pl.BlockSpec(memory_space=pl.ANY)
    vmem = pl.BlockSpec(memory_space=pltpu.VMEM)
    dma = pltpu.SemaphoreType.DMA
    dec_attn, pre_attn, appended, fresh = pl.pallas_call(
        functools.partial(step_kernel, n_tok),
        name="attention_step",
        out_shape=(
            jax.ShapeDtypeStruct((dec_rows, q_width), BF16),
            jax.ShapeDtypeStruct((pre_rows, q_width), BF16),
            jax.ShapeDtypeStruct((2, pre_rows, HD), BF16),
            jax.ShapeDtypeStruct((2, dec_rows, HD), BF16),
        ),
        in_specs=[pl.BlockSpec(memory_space=pltpu.HBM)] * 12,
        out_specs=(vmem, vmem, vmem, vmem),
        scratch_shapes=[
            pltpu.VMEM((4, dec_rows, width), BF16),
            pltpu.VMEM((4, pre_rows, width), BF16),
            pltpu.VMEM((depth, out_width), BF16),
            pltpu.VMEM((2 * depth, HD), BF16),
            pltpu.VMEM(dec_pool.shape, BF16),
            pltpu.VMEM((2, 2 * shard, HD), BF16),
            pltpu.VMEM((2, 2 * pre_rows, HD), BF16),
            pltpu.VMEM((GROUPS, heads * rows, HD), BF16),
            pltpu.VMEM((GROUPS, heads * rows, HD), F32),
            pltpu.VMEM((GROUPS, heads * rows, HD), F32),
            pltpu.VMEM((GROUPS, heads * rows, HD), F32),
            pltpu.VMEM((dec_rows, out_width), BF16),
            pltpu.VMEM((n_tok, dec_rows, out_width), BF16),
            pltpu.VMEM((n_tok, dec_rows, q_width), BF16),
            pltpu.VMEM((n_tok, dec_rows, q_width), BF16),
            pltpu.VMEM((q_width,), F32),
            pltpu.VMEM((2, HD), F32),
            pltpu.SMEM(owner_slots.shape, jnp.int32),
            pltpu.SMEM(dec_lengths.shape, jnp.int32),
            pltpu.SMEM(pre_offsets.shape, jnp.int32),
            pltpu.VMEM((1, HD), F32),
            pltpu.VMEM((rows, 2 * shard), F32),
            pltpu.VMEM((heads * dec_rows, dec_pool.shape[1]), F32),
            dma((12,)),
            dma((3,)), dma((3,)),
            dma((CHUNKS, 4)), dma((CHUNKS, 4)),
            dma((n_tok - 1,)), dma((n_tok - 1,)),
            dma((n_tok - 1,)), dma((n_tok - 1,)),
            dma, dma,
            dma((GROUPS,)), dma((GROUPS,)),
        ],
        compiler_params=pltpu.CompilerParams(
            collective_id=0, has_side_effects=True, vmem_limit_bytes=64 * 1024 * 1024
        ),
    )(
        dec_tokens, pre_tokens, w_query, w_keyval.reshape(2 * depth, HD),
        b_query, b_keyval, dec_pool, owner_slots, dec_lengths,
        pre_cache, pre_offsets, rates,
    )
    rest = (dec_attn, pre_attn, appended)
    new_pool, dec_attn, pre_attn, appended = pl.pallas_call(
        pool_kernel,
        name="append_rows",
        out_shape=(
            jax.ShapeDtypeStruct(dec_pool.shape, BF16),
            *(jax.ShapeDtypeStruct(value.shape, BF16) for value in rest),
        ),
        in_specs=[hbm] * 6,
        out_specs=[hbm] * 4,
        scratch_shapes=[
            pltpu.VMEM(dec_pool.shape, BF16),
            pltpu.VMEM(fresh.shape, BF16),
            pltpu.SMEM(dec_lengths.shape, jnp.int32),
            *(pltpu.VMEM(value.shape, BF16) for value in rest),
            dma((13,)), dma((11,)),
        ],
        compiler_params=pltpu.CompilerParams(vmem_limit_bytes=64 * 1024 * 1024),
    )(dec_pool, fresh, dec_lengths, *rest)
    return (dec_attn, pre_attn, new_pool, appended)


def solution(mesh):
    in_specs = (
        P("tok", "kv"),
        P("tok", "kv"),
        P(None, "kv"),
        P(None, None, "kv"),
        P("kv"),
        P(None, "kv"),
        P(None, "tok", "kv"),
        P("tok"),
        P("tok"),
        P(None, "tok", "kv"),
        P(),
    )
    out_specs = (P("tok", "kv"), P("tok", "kv"), P(None, "tok", "kv"), P(None, "tok", "kv"))
    return jax.shard_map(
        functools.partial(body, mesh.shape["tok"]),
        mesh=mesh, in_specs=in_specs, out_specs=out_specs, check_vma=False,
    )
```
